256 devices in a mesh: grp: 2 (over core), dev: 128 (over x, z, y).
Axes of the slice: x: 4, y: 4, z: 8, core: 2. Of those that a mesh axis runs over, the one named last changes fastest.
Arguments:
- teacher_input: bfloat16 [32768, 2048], P(('grp', 'dev')), may hold values from -6 to 6
- expert_routes: int32 [32768, 8], P(('grp', 'dev')), may hold values from 0 to 127, all different within a row; in each aligned block of 128 rows (0 to 127, 128 to 255, ...) at most 12 rows name the same one
- route_gates: float32 [32768, 8], P(('grp', 'dev')), may hold values from 0.05 to 0.3
- expert_gate_up: bfloat16 [128, 2048, 1536], P('dev'), may hold values from -0.125 to 0.125
- expert_down: bfloat16 [128, 768, 1024], P('dev'), may hold values from -0.21875 to 0.21875
- student_owner: int32 [32768], P(('grp', 'dev')), may hold values from 0 to 127, as said below
- student_input: bfloat16 [32768, 1792], P(('grp', 'dev')), may hold values from -24 to 24
- student_gain: float32 [1792], replicated, may hold values from 0.5 to 1.5
- align_weight: bfloat16 [1792, 1024], P('dev'), may hold values from -0.125 to 0.125
Outputs:
- token_loss: float32 [32768], P(('grp', 'dev'))
- input_grad: bfloat16 [32768, 1792], P(('grp', 'dev'))
- gain_grad: float32 [1792], replicated
- align_grad: float32 [1792, 1024], P('dev')
The draws below stay inside these ranges and needn't reach their ends.
Inputs may be any that keep to these rules, and one draw needn't show every extreme that they name: `expert_routes`: in each aligned block of 128 rows (the rows of one device) no expert is named by more than 12 routes, a bound that some block reaches; a row's 8 experts differ. `student_owner`: the 128 tokens of each device name every owner exactly 1 times; the owner is a device of the token's own half along grp.
All inputs are finite; a program needn't handle non-finite values.
Results may differ from the reference program's by a relative error of at most 0.013.
Values may be sent and summed in bfloat16 or wider, within the bound.
No kernel may reach another device: no remote copies, remote signals or barrier semaphores. Data moves between devices by JAX's collectives and lax.ppermute only.
A program may use at most 128 MiB of HBM per device.

```python
import math
import jax
import jax.numpy as jnp
import numpy as np
from jax import lax

DT = 2048
FE = 768
DW = 1024
DS = 1792
TOPK = 8
TOK_DEV = 128
EXPERTS = 128
CAP = 12
OWN_PER = 1
TOKENS = 32768
N_GRP = 2
N_DEV = 128


def draw_student_owner(key, part):
    key = jax.random.fold_in(key, 7)
    device_keys = jax.random.split(key, TOKENS // TOK_DEV)
    base_row = jnp.arange(TOK_DEV, dtype=jnp.int32) % EXPERTS
    permuted = jax.vmap(lambda each_key: jax.random.permutation(each_key, base_row))(device_keys)
    return permuted.reshape(-1).astype(jnp.int32)


def with_spikes(values, key, source, target, blocks, factor):
    def block_of(axis_at):
        return (jnp.arange(values.shape[axis_at]) // (values.shape[axis_at] // blocks)).reshape((-1,) + (1,) * (values.ndim - 1 - axis_at))

    one_side = jax.random.permutation(key, blocks)[block_of(target)]
    other_side = (block_of(target) + blocks // 2) % blocks
    return jnp.where((block_of(source) == one_side) | (block_of(source) == other_side), factor * values, values)


def steps_of(stream_key, dims, shards, least, largest):
    factor_of, own = 1.0, jax.random.fold_in(stream_key, 6)
    for position, parts in shards:
        draws = jnp.exp(jax.random.uniform(jax.random.fold_in(own, position), (parts,), jnp.float32, least / len(shards), largest / len(shards)))
        factor_of = factor_of * jnp.repeat(draws, dims[position] // parts).reshape([-1 if axis == position else 1 for axis in range(len(dims))])
    return factor_of


def assign_block(own_key, own, number, rows, count, top, bound, slope):
    sequence = jax.random.permutation(own_key, count)
    crowded, usual = load_shares(count, rows * top, bound, slope, True), load_shares(count, rows * top, bound, slope, False)
    places = jnp.arange(count)

    def named(lengths, turn):
        used = int((lengths > 0).sum())
        fixed = max(1, used // 4)
        shifted = fixed + (places - fixed + turn * (used - fixed)) % max(1, count - fixed)
        return jnp.zeros((count,), jnp.int32).at[sequence[jnp.where(places < fixed, places, shifted)]].set(jnp.asarray(lengths, jnp.int32))

    lengths = jnp.where(number % 4 == 0, named(crowded, number // 4), named(usual, number - number // 4 - 1))
    mixed = jax.random.permutation(jax.random.fold_in(own, 3), count)
    donor, sink = mixed[0:count // 2 * 2:2], mixed[1:count // 2 * 2:2]
    slack = jnp.minimum(lengths[donor] - 1, bound - lengths[sink]) // 2
    slack = jnp.where((donor == sequence[0]) | (sink == sequence[0]) | (lengths[sink] == 0), 0, jnp.maximum(slack, 0))
    shifted = jax.random.randint(jax.random.fold_in(own, 4), (count // 2,), 0, 1 << 20) % (slack + 1)
    lengths = lengths.at[donor].add(-shifted).at[sink].add(shifted)
    labels = jnp.searchsorted(jnp.cumsum(lengths), jnp.arange(rows * top), side="right").astype(jnp.int32)
    table = labels.reshape(top, rows).T
    table = table[jax.random.permutation(jax.random.fold_in(own, 1), rows)]
    turn = jax.random.randint(jax.random.fold_in(own, 2), (rows, 1), 0, top)
    return jnp.take_along_axis(table, (jnp.arange(top)[None, :] + turn) % top, axis=1)


def load_shares(amount, total, reach, lean, full):
    portions = [(1 << 20) // math.isqrt(standing ** lean) + 1 for standing in range(1, amount + 1)]
    largest = reach if full else min(reach, max(-(-total // amount), total * portions[0] // sum(portions)))
    least = 1 if total - largest >= amount - 1 else 0
    holding, spare = [largest] + [least] * (amount - 1), total - largest - least * (amount - 1)
    while spare > 0:
        candidates = [i for i in range(1, amount) if holding[i] < largest] or [i for i in range(1, amount) if holding[i] < reach]
        mass, left = sum([portions[i] for i in candidates]), spare
        for i in candidates:
            extra = min(reach - holding[i], max(1, left * portions[i] // mass), spare)
            holding[i] = holding[i] + extra
            spare = spare - extra
    return np.array(holding)


def centred(own_key, extent, scale, reach, pieces=(), kind=jnp.bfloat16):
    factor_of = steps_of(own_key, extent, pieces, -0.22, 0.18) if pieces else 1.0
    array = jax.random.normal(own_key, extent, jnp.float32) * scale * factor_of
    return jnp.minimum(jnp.maximum(array, -reach), reach).astype(kind)


def gaussian_with(rng, shape, deviation, most, pieces, heavy, held_as=jnp.bfloat16):
    drawn = deviation * jax.random.normal(rng, shape, jnp.float32)
    if pieces:
        drawn = drawn * steps_of(rng, shape, pieces, -0.22, 0.18)
    return jnp.clip(with_spikes(drawn, jax.random.fold_in(rng, 3), *heavy), -most, most).astype(held_as)


def setup_inputs(seed: int = 0) -> dict:
    key_list = jax.random.split(jax.random.key(seed), 10)
    teacher_input = centred(key_list[0], (TOKENS, DT), 1.0, 6.0, ((0, 256),))
    expert_routes_keys = jax.random.split(jax.random.fold_in(key_list[1], 1), TOKENS // TOK_DEV)
    expert_routes_turns = jax.random.permutation(jax.random.fold_in(key_list[1], 3), TOKENS // TOK_DEV)
    expert_routes = jax.vmap(lambda own, number: assign_block(jax.random.fold_in(key_list[1], 2), own, number, TOK_DEV, EXPERTS, TOPK, CAP, 2))(expert_routes_keys, expert_routes_turns).reshape((TOKENS, TOPK))
    route_gates = jnp.clip(0.05 + 0.25 * jax.random.uniform(key_list[2], (TOKENS, TOPK), jnp.float32) ** steps_of(key_list[2], (TOKENS, TOPK), ((0, 256),), -0.2, 0.2), 0.05, 0.3)
    expert_gate_up = centred(key_list[3], (EXPERTS, DT, 2 * FE), DT ** -0.5, 0.125, ((0, 128),))
    expert_down = centred(key_list[4], (EXPERTS, FE, DW), FE ** -0.5, 0.21875, ((0, 128),))
    student_owner = draw_student_owner(jax.random.fold_in(key_list[9], 71), 0)
    student_input = gaussian_with(key_list[6], (TOKENS, DS), 1.0, 24.0, ((0, 256),), (0, 1, 256, 6.0))
    student_gain = jnp.clip(1.0 + 0.1 * jax.random.normal(key_list[7], (DS,), jnp.float32), 0.5, 1.5)
    align_weight = centred(key_list[8], (DS, DW), DS ** -0.5, 0.125, ((0, 128),))
    return {"teacher_input": teacher_input, "expert_routes": expert_routes, "route_gates": route_gates, "expert_gate_up": expert_gate_up, "expert_down": expert_down, "student_owner": student_owner, "student_input": student_input, "student_gain": student_gain, "align_weight": align_weight}


epsilon = 1e-06

def expert_rows(inputs, gate_up, down_proj):
    hidden_both = jnp.dot(inputs, gate_up, preferred_element_type=jnp.float32)
    split_at = gate_up.shape[1] // 2
    hidden = (jax.nn.silu(hidden_both[:, :split_at]) * hidden_both[:, split_at:]).astype(jnp.bfloat16)
    return jnp.dot(hidden, down_proj, preferred_element_type=jnp.float32).astype(jnp.bfloat16)

def row_scale(values):
    return lax.rsqrt(lax.optimization_barrier(jnp.mean(values * values, axis=-1, keepdims=True)) + epsilon)

def reference(teacher_input, expert_routes, route_gates, expert_gate_up, expert_down, student_owner, student_input, student_gain, align_weight):
    flat_routes = expert_routes.reshape(-1)
    flat_gates = route_gates.reshape(-1)
    pair_count = TOKENS * TOPK
    row_limit = N_GRP * N_DEV * CAP

    def one_expert(running, inputs):
        expert_id, gate_up, down_proj = inputs
        chosen = jnp.nonzero(flat_routes == expert_id, size=row_limit, fill_value=pair_count)[0].astype(jnp.int32)
        in_range = chosen < pair_count
        safe_tokens = jnp.minimum(chosen // TOPK, TOKENS - 1).astype(jnp.int32)
        produced = expert_rows(teacher_input[safe_tokens], gate_up, down_proj)
        gate_vals = jnp.where(in_range, flat_gates[jnp.minimum(chosen, pair_count - 1)], jnp.zeros((), jnp.float32))
        running = running.at[safe_tokens].add(gate_vals[:, None] * produced.astype(jnp.float32))
        return (running, None)
    teacher_out, unused = lax.scan(one_expert, jnp.zeros((TOKENS, DW), jnp.float32), (jnp.arange(EXPERTS, dtype=jnp.int32), expert_gate_up, expert_down))
    teacher_target = (teacher_out * row_scale(teacher_out)).astype(jnp.bfloat16)
    owner_rows = student_owner.reshape(-1, TOK_DEV)
    owner_hot = (owner_rows[:, :, None] == jnp.arange(N_DEV, dtype=jnp.int32)[None, None, :]).astype(jnp.int32)
    owner_rank = lax.optimization_barrier(jnp.sum((jnp.cumsum(owner_hot, axis=1) - owner_hot) * owner_hot, axis=-1))
    source_dev = jnp.arange(owner_rows.shape[0], dtype=jnp.int32)[:, None]
    grp_index = source_dev // N_DEV
    dev_index = source_dev % N_DEV
    destination = ((grp_index * N_DEV + owner_rows) * TOK_DEV + dev_index * OWN_PER + owner_rank).astype(jnp.int32)
    student_target = jnp.zeros((TOKENS, DW), jnp.bfloat16).at[destination.reshape(-1)].set(teacher_target)
    inputs_f = student_input.astype(jnp.float32)
    scale_rows = row_scale(inputs_f)
    unit_rows = inputs_f * scale_rows
    normed = (unit_rows * student_gain).astype(jnp.bfloat16)
    student_out = jnp.dot(normed, align_weight, preferred_element_type=jnp.float32)
    distance = student_out - student_target.astype(jnp.float32)
    token_loss = lax.optimization_barrier(jnp.mean(distance * distance, axis=-1))
    distance_bf = distance.astype(jnp.bfloat16)
    normed_grad = lax.dot_general(distance_bf, align_weight, (((1,), (1,)), ((), ())), preferred_element_type=jnp.float32)
    gain_inner = normed_grad * student_gain
    input_grad = (scale_rows * (gain_inner - unit_rows * lax.optimization_barrier(jnp.mean(gain_inner * unit_rows, axis=-1, keepdims=True)))).astype(jnp.bfloat16)
    grad_factor = 1.0 / math.sqrt(TOKENS)
    gain_grad = lax.optimization_barrier(jnp.sum(normed_grad * unit_rows, axis=0)) * grad_factor
    align_grad = lax.dot_general(normed, distance_bf, (((0,), (0,)), ((), ())), preferred_element_type=jnp.float32) * grad_factor
    return (token_loss, input_grad, gain_grad, align_grad)
```

```python
import math

import jax
import jax.numpy as jnp
from jax import lax
from jax.sharding import Mesh
from jax.sharding import PartitionSpec as P

epsilon = 1e-06
DEV = ("x", "z", "y")
DEV_SHAPE = (4, 8, 4)
SWAP = ((0, 1), (1, 0))


def expert_rows(inputs, gate_up, down_proj):
    hidden_both = jnp.dot(inputs, gate_up, preferred_element_type=jnp.float32)
    split_at = gate_up.shape[1] // 2
    hidden = (jax.nn.silu(hidden_both[:, :split_at]) * hidden_both[:, split_at:]).astype(
        jnp.bfloat16
    )
    return jnp.dot(hidden, down_proj, preferred_element_type=jnp.float32).astype(jnp.bfloat16)


def row_scale(values):
    return lax.rsqrt(jnp.mean(values * values, axis=-1, keepdims=True) + epsilon)


def rank_within(labels, label_count):
    label_hot = (labels[:, None] == jnp.arange(label_count, dtype=jnp.int32)[None, :]).astype(
        jnp.int32
    )
    earlier = jnp.cumsum(label_hot, axis=0) - label_hot
    return jnp.sum(earlier * label_hot, axis=1)


def body(
    teacher_input,
    expert_routes,
    route_gates,
    expert_gate_up,
    expert_down,
    student_owner,
    student_input,
    student_gain,
    align_weight,
):
    tok_rows = teacher_input.shape[0]
    top_count = expert_routes.shape[1]
    width_in = teacher_input.shape[1]
    owner_count = lax.axis_size(DEV)
    capacity = 3 * tok_rows * top_count // (2 * owner_count)
    pair_count = tok_rows * top_count
    flat_routes = expert_routes.reshape(-1)
    route_slot = rank_within(flat_routes, owner_count)
    slot_place = flat_routes * capacity + route_slot
    slot_table = (
        jnp.full((owner_count * capacity,), pair_count, jnp.int32)
        .at[slot_place]
        .set(jnp.arange(pair_count, dtype=jnp.int32))
    )
    padded = jnp.concatenate([teacher_input, jnp.zeros((1, width_in), teacher_input.dtype)], axis=0)
    source_rows = jnp.where(slot_table < pair_count, slot_table // top_count, tok_rows)
    outgoing = padded[source_rows].reshape(owner_count, capacity, width_in)
    gate_up = expert_gate_up[0]
    down_proj = expert_down[0]
    arrived = lax.all_to_all(outgoing, DEV, split_axis=0, concat_axis=0, tiled=True)
    senders = arrived.shape[0]
    slot_count = arrived.shape[1]
    produced = expert_rows(arrived.reshape(senders * slot_count, width_in), gate_up, down_proj)
    produced = produced.reshape(senders, slot_count, down_proj.shape[1])
    returned = lax.all_to_all(produced, DEV, split_axis=0, concat_axis=0, tiled=True)
    picked = returned.reshape(owner_count * capacity, -1)[slot_place].reshape(
        tok_rows, top_count, -1
    )
    teacher_out = jnp.einsum("tk,tkd->td", route_gates, picked.astype(jnp.float32))
    teacher_target = (teacher_out * row_scale(teacher_out)).astype(jnp.bfloat16)
    per_owner = tok_rows // owner_count
    owner_place = student_owner * per_owner + rank_within(student_owner, owner_count)
    inverse = (
        jnp.zeros((tok_rows,), jnp.int32).at[owner_place].set(jnp.arange(tok_rows, dtype=jnp.int32))
    )
    relay_rows = teacher_target[inverse].reshape(owner_count, per_owner, -1)
    student_target = lax.all_to_all(
        relay_rows, DEV, split_axis=0, concat_axis=0, tiled=True
    ).reshape(tok_rows, -1)
    full_weight = lax.all_gather(align_weight, DEV, axis=0, tiled=True)
    inputs_f = student_input.astype(jnp.float32)
    scale_rows = row_scale(inputs_f)
    unit_rows = inputs_f * scale_rows
    normed = (unit_rows * student_gain).astype(jnp.bfloat16)
    student_out = jnp.dot(normed, full_weight, preferred_element_type=jnp.float32)
    size_x, size_z, size_y = (lax.axis_size(name) for name in DEV)
    shard_rows = align_weight.shape[0]
    normed_z = (
        normed.reshape(tok_rows, size_x, size_z, size_y * shard_rows)
        .transpose(0, 2, 1, 3)
        .reshape(tok_rows, -1)
    )
    normed_pair = jnp.concatenate([normed_z, lax.ppermute(normed_z, "grp", SWAP)], axis=0)
    distance = student_out - student_target.astype(jnp.float32)
    token_loss = jnp.mean(distance * distance, axis=-1)
    distance_bf = distance.astype(jnp.bfloat16)
    core = lax.axis_index("grp")
    half = distance_bf.shape[1] // 2
    low, high = distance_bf[:, :half], distance_bf[:, half:]
    kept = jnp.where(core == 0, low, high)
    given = jnp.where(core == 0, high, low)
    distance_pair = jnp.concatenate([kept, lax.ppermute(given, "grp", SWAP)], axis=0)
    term = lax.dot_general(
        normed_pair, distance_pair, (((0,), (0,)), ((), ())), preferred_element_type=jnp.float32
    ).astype(jnp.bfloat16)
    term = lax.psum_scatter(term, "z", scatter_dimension=0, tiled=True)
    term = term.reshape(size_x * size_y, shard_rows, half)
    term = lax.all_to_all(term, ("x", "y"), split_axis=0, concat_axis=0, tiled=True)
    tokens_all = tok_rows * lax.axis_size("grp") * owner_count
    grad_factor = 1.0 / math.sqrt(tokens_all)
    shard_half = jnp.sum(term.astype(jnp.float32), axis=0) * grad_factor
    other_half = lax.ppermute(shard_half, "grp", SWAP)
    align_grad = jnp.where(
        core == 0,
        jnp.concatenate([shard_half, other_half], axis=1),
        jnp.concatenate([other_half, shard_half], axis=1),
    )
    normed_grad = lax.dot_general(
        distance_bf, full_weight, (((1,), (1,)), ((), ())), preferred_element_type=jnp.float32
    )
    gain_inner = normed_grad * student_gain
    input_grad = (
        scale_rows
        * (gain_inner - unit_rows * jnp.mean(gain_inner * unit_rows, axis=-1, keepdims=True))
    ).astype(jnp.bfloat16)
    gain_part = jnp.sum(normed_grad * unit_rows, axis=0)
    gain_part = jnp.sum(lax.all_gather(gain_part, ("grp", "z"), axis=0), axis=0)
    gain_part = jnp.sum(lax.all_gather(gain_part, ("x", "y"), axis=0), axis=0)
    gain_grad = gain_part * grad_factor
    return (token_loss, input_grad, gain_grad, align_grad)


def solution(mesh):
    grid = Mesh(mesh.devices.reshape((mesh.devices.shape[0],) + DEV_SHAPE), ("grp",) + DEV)
    tokens = ("grp",) + DEV
    placed = (
        P(tokens, None),
        P(tokens, None),
        P(tokens, None),
        P(DEV, None, None),
        P(DEV, None, None),
        P(tokens),
        P(tokens, None),
        P(),
        P(DEV, None),
    )
    return jax.shard_map(
        body,
        mesh=grid,
        in_specs=placed,
        out_specs=(P(tokens), P(tokens, None), P(), P(DEV, None)),
        check_vma=False,
    )
```

```python
import math

import jax
import jax.numpy as jnp
from jax import lax
from jax.sharding import Mesh
from jax.sharding import PartitionSpec as P

epsilon = 1e-06
DEV = ("x", "z", "y")
DEV_SHAPE = (4, 8, 4)
SWAP = ((0, 1), (1, 0))
GROUPS = ((0, 1), (-1, 2, -2, 3), (-3, 4))


def shifts(count, by):
    return [(i, (i + by) % count) for i in range(count)]


def expert_rows(inputs, gate_up, down_proj):
    hidden_both = jnp.dot(inputs, gate_up, preferred_element_type=jnp.float32)
    split_at = gate_up.shape[1] // 2
    hidden = (jax.nn.silu(hidden_both[:, :split_at]) * hidden_both[:, split_at:]).astype(
        jnp.bfloat16
    )
    return jnp.dot(hidden, down_proj, preferred_element_type=jnp.float32).astype(jnp.bfloat16)


def row_scale(values):
    return lax.rsqrt(jnp.mean(values * values, axis=-1, keepdims=True) + epsilon)


def rank_within(labels, label_count):
    label_hot = (labels[:, None] == jnp.arange(label_count, dtype=jnp.int32)[None, :]).astype(
        jnp.int32
    )
    earlier = jnp.cumsum(label_hot, axis=0) - label_hot
    return jnp.sum(earlier * label_hot, axis=1)


def body(
    teacher_input,
    expert_routes,
    route_gates,
    expert_gate_up,
    expert_down,
    student_owner,
    student_input,
    student_gain,
    align_weight,
):
    tok_rows = teacher_input.shape[0]
    top_count = expert_routes.shape[1]
    owner_count = lax.axis_size(DEV)
    gate_up = expert_gate_up[0]
    down_proj = expert_down[0]
    size_x, size_z, size_y = (lax.axis_size(name) for name in DEV)
    plane = lax.axis_index("z")
    capacity = 3 * tok_rows * top_count // (2 * owner_count)

    held = {0: teacher_input}
    for step in range(1, size_z // 2 + 1):
        held[step] = lax.ppermute(held[step - 1], "z", shifts(size_z, -1))
        if step > 1:
            held[1 - step] = lax.ppermute(held[2 - step], "z", shifts(size_z, 1))

    info = jnp.concatenate([expert_routes.T.astype(jnp.float32), route_gates.T], axis=0)
    info = lax.all_gather(info, "z", axis=0)
    info = lax.dynamic_slice_in_dim(jnp.concatenate([info, info], axis=0), plane, size_z, axis=0)
    expert_ids = (
        jnp.arange(size_x)[:, None] * (size_z * size_y) + plane * size_y + jnp.arange(size_y)[None, :]
    ).reshape(-1)
    named = info[:, None, :top_count, :] == expert_ids.astype(jnp.float32)[None, :, None, None]
    chosen = jnp.any(named, axis=2)
    gate_of = jnp.sum(jnp.where(named, info[:, None, top_count:, :], 0.0), axis=2)
    before = (jnp.arange(tok_rows)[:, None] < jnp.arange(tok_rows)[None, :]).astype(jnp.bfloat16)
    rank = jnp.dot(chosen.astype(jnp.bfloat16), before, preferred_element_type=jnp.float32)
    slot = jnp.where(chosen, rank.astype(jnp.int32), -size_z * capacity)
    plane_experts = size_x * size_y
    width_in = teacher_input.shape[1]
    width_out = down_proj.shape[1]

    teacher_out = jnp.zeros((tok_rows, width_out), jnp.float32)
    for group in GROUPS:
        count = len(group)
        slots = count * capacity
        places = [offset % size_z for offset in group]
        spot = jnp.concatenate([slot[q] + n * capacity for n, q in enumerate(places)], axis=1)
        gates = jnp.concatenate([gate_of[q] for q in places], axis=1)
        hot = spot[:, None, :] == jnp.arange(slots)[None, :, None]
        pick = hot.astype(jnp.bfloat16).reshape(plane_experts * slots, count * tok_rows)
        feats = jnp.concatenate([held[offset] for offset in group], axis=0)
        outgoing = jnp.dot(pick, feats, preferred_element_type=jnp.float32).astype(jnp.bfloat16)
        arrived = lax.all_to_all(
            outgoing.reshape(plane_experts, slots, width_in),
            ("x", "y"), split_axis=0, concat_axis=0, tiled=True,
        )
        produced = expert_rows(arrived.reshape(-1, width_in), gate_up, down_proj)
        returned = lax.all_to_all(
            produced.reshape(plane_experts, slots, width_out),
            ("x", "y"), split_axis=0, concat_axis=0, tiled=True,
        ).reshape(-1, width_out)
        weights = jnp.where(hot, gates[:, None, :], 0.0).reshape(pick.shape)
        coarse = weights.astype(jnp.bfloat16)
        fine = (weights - coarse.astype(jnp.float32)).astype(jnp.bfloat16)
        summed = sum(
            lax.dot_general(
                term, returned, (((0,), (0,)), ((), ())), preferred_element_type=jnp.float32
            )
            for term in (coarse, fine)
        )
        for n, offset in enumerate(group):
            part = summed[n * tok_rows : (n + 1) * tok_rows]
            if offset:
                part = lax.ppermute(
                    part.astype(jnp.bfloat16), "z", shifts(size_z, offset)
                ).astype(jnp.float32)
            teacher_out = teacher_out + part
    teacher_target = (teacher_out * row_scale(teacher_out)).astype(jnp.bfloat16)
    per_owner = tok_rows // owner_count
    owner_place = student_owner * per_owner + rank_within(student_owner, owner_count)
    inverse = (
        jnp.zeros((tok_rows,), jnp.int32).at[owner_place].set(jnp.arange(tok_rows, dtype=jnp.int32))
    )
    relay_rows = teacher_target[inverse].reshape(owner_count, per_owner, -1)
    student_target = lax.all_to_all(
        relay_rows, DEV, split_axis=0, concat_axis=0, tiled=True
    ).reshape(tok_rows, -1)
    full_weight = lax.all_gather(align_weight, DEV, axis=0, tiled=True)
    inputs_f = student_input.astype(jnp.float32)
    scale_rows = row_scale(inputs_f)
    unit_rows = inputs_f * scale_rows
    normed = (unit_rows * student_gain).astype(jnp.bfloat16)
    student_out = jnp.dot(normed, full_weight, preferred_element_type=jnp.float32)
    shard_rows = align_weight.shape[0]
    normed_z = (
        normed.reshape(tok_rows, size_x, size_z, size_y * shard_rows)
        .transpose(0, 2, 1, 3)
        .reshape(tok_rows, -1)
    )
    normed_pair = jnp.concatenate([normed_z, lax.ppermute(normed_z, "grp", SWAP)], axis=0)
    distance = student_out - student_target.astype(jnp.float32)
    token_loss = jnp.mean(distance * distance, axis=-1)
    distance_bf = distance.astype(jnp.bfloat16)
    core = lax.axis_index("grp")
    half = distance_bf.shape[1] // 2
    low, high = distance_bf[:, :half], distance_bf[:, half:]
    kept = jnp.where(core == 0, low, high)
    given = jnp.where(core == 0, high, low)
    distance_pair = jnp.concatenate([kept, lax.ppermute(given, "grp", SWAP)], axis=0)
    term = lax.dot_general(
        normed_pair, distance_pair, (((0,), (0,)), ((), ())), preferred_element_type=jnp.float32
    ).astype(jnp.bfloat16)
    term = lax.psum_scatter(term, "z", scatter_dimension=0, tiled=True)
    term = term.reshape(size_x * size_y, shard_rows, half)
    term = lax.all_to_all(term, ("x", "y"), split_axis=0, concat_axis=0, tiled=True)
    tokens_all = tok_rows * lax.axis_size("grp") * owner_count
    grad_factor = 1.0 / math.sqrt(tokens_all)
    shard_half = jnp.sum(term.astype(jnp.float32), axis=0) * grad_factor
    other_half = lax.ppermute(shard_half, "grp", SWAP)
    align_grad = jnp.where(
        core == 0,
        jnp.concatenate([shard_half, other_half], axis=1),
        jnp.concatenate([other_half, shard_half], axis=1),
    )
    normed_grad = lax.dot_general(
        distance_bf, full_weight, (((1,), (1,)), ((), ())), preferred_element_type=jnp.float32
    )
    gain_inner = normed_grad * student_gain
    input_grad = (
        scale_rows
        * (gain_inner - unit_rows * jnp.mean(gain_inner * unit_rows, axis=-1, keepdims=True))
    ).astype(jnp.bfloat16)
    gain_part = jnp.sum(normed_grad * unit_rows, axis=0)
    gain_part = jnp.sum(lax.all_gather(gain_part, ("grp", "z"), axis=0), axis=0)
    gain_part = jnp.sum(lax.all_gather(gain_part, ("x", "y"), axis=0), axis=0)
    gain_grad = gain_part * grad_factor
    return (token_loss, input_grad, gain_grad, align_grad)


def solution(mesh):
    grid = Mesh(mesh.devices.reshape((mesh.devices.shape[0],) + DEV_SHAPE), ("grp",) + DEV)
    tokens = ("grp",) + DEV
    placed = (
        P(tokens, None),
        P(tokens, None),
        P(tokens, None),
        P(DEV, None, None),
        P(DEV, None, None),
        P(tokens),
        P(tokens, None),
        P(),
        P(DEV, None),
    )
    return jax.shard_map(
        body,
        mesh=grid,
        in_specs=placed,
        out_specs=(P(tokens), P(tokens, None), P(), P(DEV, None)),
        check_vma=False,
    )
```

```python
import math

import jax
import jax.numpy as jnp
from jax import lax
from jax.sharding import Mesh
from jax.sharding import PartitionSpec as P

epsilon = 1e-06
DEV = ("x", "z", "y")
DEV_SHAPE = (4, 8, 4)
SWAP = ((0, 1), (1, 0))
GROUPS = ((0, 1, -1, 2), (-2, 3, -3, 4))


def shifts(count, by):
    return [(i, (i + by) % count) for i in range(count)]


def expert_rows(inputs, gate_up, down_proj):
    hidden_both = jnp.dot(inputs, gate_up, preferred_element_type=jnp.float32)
    split_at = gate_up.shape[1] // 2
    hidden = (jax.nn.silu(hidden_both[:, :split_at]) * hidden_both[:, split_at:]).astype(
        jnp.bfloat16
    )
    return jnp.dot(hidden, down_proj, preferred_element_type=jnp.float32).astype(jnp.bfloat16)


def row_scale(values):
    return lax.rsqrt(jnp.mean(values * values, axis=-1, keepdims=True) + epsilon)


def one_hot(index, count):
    return (index[:, None] == jnp.arange(count, dtype=index.dtype)[None, :]).astype(jnp.bfloat16)


def dot_f32(left, right):
    return jnp.dot(left, right, preferred_element_type=jnp.float32)


def body(
    teacher_input,
    expert_routes,
    route_gates,
    expert_gate_up,
    expert_down,
    student_owner,
    student_input,
    student_gain,
    align_weight,
):
    tok_rows, width_in = teacher_input.shape
    top_count = expert_routes.shape[1]
    size_x, size_z, size_y = (lax.axis_size(name) for name in DEV)
    owner_count = size_x * size_z * size_y
    plane_size = size_x * size_y
    plane = lax.axis_index("z")
    capacity = 3 * tok_rows * top_count // (2 * owner_count)
    gate_up = expert_gate_up[0]
    down_proj = expert_down[0]
    width_out = down_proj.shape[1]

    gate_rows = route_gates.T
    coarse_rows = gate_rows.astype(jnp.bfloat16)
    fine_rows = (gate_rows - coarse_rows.astype(jnp.float32)).astype(jnp.bfloat16)
    owner_rows = jnp.broadcast_to(student_owner[None, :], (top_count, tok_rows))
    notes = jnp.concatenate(
        [
            expert_routes.T.astype(jnp.bfloat16),
            coarse_rows,
            fine_rows,
            owner_rows.astype(jnp.bfloat16),
        ],
        axis=1,
    )
    notes = jnp.pad(notes, ((0, 0), (0, width_in - notes.shape[1])))
    held = {0: jnp.concatenate([teacher_input, notes], axis=0)}
    for step in range(1, size_z // 2 + 1):
        held[step] = lax.ppermute(held[step - 1], "z", shifts(size_z, -1))
        if step > 1:
            held[1 - step] = lax.ppermute(held[2 - step], "z", shifts(size_z, 1))

    full_weight = lax.all_gather(align_weight, DEV, axis=0, tiled=True)
    inputs_f = student_input.astype(jnp.float32)
    scale_rows = row_scale(inputs_f)
    unit_rows = inputs_f * scale_rows
    normed = (unit_rows * student_gain).astype(jnp.bfloat16)
    student_out = dot_f32(normed, full_weight)
    shard_rows = align_weight.shape[0]
    normed_xy = (
        normed.reshape(tok_rows, size_x, size_z, size_y, shard_rows)
        .transpose(0, 1, 3, 2, 4)
        .reshape(tok_rows, -1)
    )
    normed_pair = jnp.concatenate([normed_xy, lax.ppermute(normed_xy, "grp", SWAP)], axis=0)

    expert_ids = (
        jnp.arange(size_x)[:, None] * (size_z * size_y)
        + plane * size_y
        + jnp.arange(size_y)[None, :]
    ).reshape(-1)
    teacher_out = jnp.zeros((tok_rows, width_out), jnp.float32)
    for number, group in enumerate(GROUPS):
        count = len(group)
        slots = count * capacity
        columns = count * tok_rows
        feats = jnp.concatenate([held[offset][:tok_rows] for offset in group], axis=0)
        routes, coarse, fine, owners = (
            jnp.concatenate(
                [
                    held[offset][tok_rows:, part * tok_rows : (part + 1) * tok_rows]
                    for offset in group
                ],
                axis=1,
            )
            for part in range(4)
        )
        named = routes.astype(jnp.int32)[None, :, :] == expert_ids[:, None, None]
        chosen = jnp.any(named, axis=1)
        at = jnp.arange(columns)
        before = (at[:, None] < at[None, :]) & (at[:, None] // tok_rows == at[None, :] // tok_rows)
        rank = dot_f32(chosen.astype(jnp.bfloat16), before.astype(jnp.bfloat16))
        first = (at // tok_rows * capacity + 1).astype(jnp.float32)
        spot = jnp.where(chosen, rank + first[None, :], 0.0)
        coarse = jnp.sum(jnp.where(named, coarse[None].astype(jnp.float32), 0.0), axis=1)
        fine = jnp.sum(jnp.where(named, fine[None].astype(jnp.float32), 0.0), axis=1)
        numbers = jnp.arange(1, slots + 1).astype(jnp.float32)[None, :, None]
        pick = (spot[:, None, :] == numbers).astype(jnp.bfloat16).reshape(-1, columns)
        outgoing = dot_f32(pick, feats).astype(jnp.bfloat16)
        arrived = lax.all_to_all(
            outgoing.reshape(plane_size, slots, width_in),
            ("x", "y"),
            split_axis=0,
            concat_axis=0,
            tiled=True,
        )
        produced = expert_rows(arrived.reshape(-1, width_in), gate_up, down_proj)
        if number == len(GROUPS) - 1:
            produced, student_out, normed_pair = lax.optimization_barrier(
                (produced, student_out, normed_pair)
            )
        returned = lax.all_to_all(
            produced.reshape(plane_size, slots, width_out),
            ("x", "y"),
            split_axis=0,
            concat_axis=0,
            tiled=True,
        ).reshape(-1, width_out)
        owner = owners[0].astype(jnp.int32)
        ahead = (owner // size_y - plane) % size_z
        within = owner // (size_y * size_z) * size_y + owner % size_y
        goes = ahead * (count * plane_size) + at // tok_rows * plane_size + within
        moved = dot_f32(
            jnp.concatenate([spot, coarse, fine], axis=0).astype(jnp.bfloat16),
            one_hot(goes, columns),
        )
        spot, coarse, fine = jnp.split(moved, 3, axis=0)
        hot = spot[:, None, :] == numbers
        summed = sum(
            lax.dot_general(
                jnp.where(hot, term[:, None, :], 0.0).astype(jnp.bfloat16).reshape(-1, columns),
                returned,
                (((0,), (0,)), ((), ())),
                preferred_element_type=jnp.float32,
            )
            for term in (coarse, fine)
        ).astype(jnp.bfloat16)
        block = count * plane_size
        parts = [summed[:block]] + [
            lax.ppermute(summed[by * block : (by + 1) * block], "z", shifts(size_z, by))
            for by in range(1, size_z)
        ]
        source = [
            within * size_z + (offset - by) % size_z
            for by in range(size_z)
            for offset in group
            for within in range(plane_size)
        ]
        gather = one_hot(jnp.array(source, jnp.int32), tok_rows)
        teacher_out = teacher_out + lax.dot_general(
            gather,
            jnp.concatenate(parts, axis=0),
            (((0,), (0,)), ((), ())),
            preferred_element_type=jnp.float32,
        )
    teacher_target = (teacher_out * row_scale(teacher_out)).astype(jnp.bfloat16)
    relayed = lax.all_to_all(
        teacher_target.reshape(plane_size, size_z, width_out),
        ("x", "y"),
        split_axis=0,
        concat_axis=0,
        tiled=True,
    ).reshape(tok_rows, width_out)
    at = jnp.arange(tok_rows)
    place = (at // (size_z * size_y) * size_y + at % size_y) * size_z + (
        at // size_y - plane
    ) % size_z
    student_target = dot_f32(one_hot(place, tok_rows), relayed)

    distance = student_out - student_target
    token_loss = jnp.mean(distance * distance, axis=-1)
    distance_bf = distance.astype(jnp.bfloat16)
    core = lax.axis_index("grp")
    half = width_out // 2
    low, high = distance_bf[:, :half], distance_bf[:, half:]
    kept = jnp.where(core == 0, low, high)
    given = jnp.where(core == 0, high, low)
    distance_pair = jnp.concatenate([kept, lax.ppermute(given, "grp", SWAP)], axis=0)
    term = lax.dot_general(
        normed_pair, distance_pair, (((0,), (0,)), ((), ())), preferred_element_type=jnp.float32
    ).astype(jnp.bfloat16)
    term = lax.all_to_all(
        term.reshape(plane_size, size_z * shard_rows, half),
        ("x", "y"),
        split_axis=0,
        concat_axis=0,
        tiled=True,
    )
    term = jnp.sum(term.astype(jnp.float32), axis=0).reshape(size_z, shard_rows, half)

    normed_grad = lax.dot_general(
        distance_bf, full_weight, (((1,), (1,)), ((), ())), preferred_element_type=jnp.float32
    )
    gain_inner = normed_grad * student_gain
    input_grad = (
        scale_rows
        * (gain_inner - unit_rows * jnp.mean(gain_inner * unit_rows, axis=-1, keepdims=True))
    ).astype(jnp.bfloat16)
    gain_part = jnp.sum(normed_grad * unit_rows, axis=0)
    gain_part = jnp.sum(lax.all_gather(gain_part, ("x", "y"), axis=0), axis=0)

    gain_size = gain_part.shape[0]
    gain_rows = -(-gain_size // half)
    gain_part = jnp.pad(gain_part, (0, gain_rows * half - gain_size)).reshape(1, gain_rows, half)
    term = jnp.concatenate(
        [term, jnp.broadcast_to(gain_part, (size_z, gain_rows, half))], axis=1
    )
    term = jnp.sum(
        lax.all_to_all(term, "z", split_axis=0, concat_axis=0, tiled=True), axis=0
    )
    other = lax.ppermute(term, "grp", SWAP)
    grad_factor = 1.0 / math.sqrt(tok_rows * lax.axis_size("grp") * owner_count)
    gain_grad = (term + other)[shard_rows:].reshape(-1)[:gain_size] * grad_factor
    term, other = term[:shard_rows] * grad_factor, other[:shard_rows] * grad_factor
    align_grad = jnp.where(
        core == 0,
        jnp.concatenate([term, other], axis=1),
        jnp.concatenate([other, term], axis=1),
    )
    return (token_loss, input_grad, gain_grad, align_grad)


def solution(mesh):
    grid = Mesh(mesh.devices.reshape((mesh.devices.shape[0],) + DEV_SHAPE), ("grp",) + DEV)
    tokens = ("grp",) + DEV
    placed = (
        P(tokens, None),
        P(tokens, None),
        P(tokens, None),
        P(DEV, None, None),
        P(DEV, None, None),
        P(tokens),
        P(tokens, None),
        P(),
        P(DEV, None),
    )
    return jax.shard_map(
        body,
        mesh=grid,
        in_specs=placed,
        out_specs=(P(tokens), P(tokens, None), P(), P(DEV, None)),
        check_vma=False,
    )
```

```python
import math

import jax
import jax.numpy as jnp
from jax import lax
from jax.sharding import Mesh
from jax.sharding import PartitionSpec as P

epsilon = 1e-06
DEV = ("x", "z", "y")
DEV_SHAPE = (4, 8, 4)
SWAP = ((0, 1), (1, 0))
GROUPS = (((0, 1), (-1, 2)), ((-2, 3, -3, 4),))


def shifts(count, by):
    return [(i, (i + by) % count) for i in range(count)]


def expert_rows(inputs, gate_up, down_proj):
    hidden_both = jnp.dot(inputs, gate_up, preferred_element_type=jnp.float32)
    split_at = gate_up.shape[1] // 2
    hidden = (jax.nn.silu(hidden_both[:, :split_at]) * hidden_both[:, split_at:]).astype(
        jnp.bfloat16
    )
    return jnp.dot(hidden, down_proj, preferred_element_type=jnp.float32).astype(jnp.bfloat16)


def row_scale(values):
    return lax.rsqrt(jnp.mean(values * values, axis=-1, keepdims=True) + epsilon)


def one_hot(index, count):
    return (index[:, None] == jnp.arange(count, dtype=index.dtype)[None, :]).astype(jnp.bfloat16)


def dot_f32(left, right):
    return jnp.dot(left, right, preferred_element_type=jnp.float32)


def dot_t(left, right, dims):
    return lax.dot_general(left, right, ((dims, dims), ((), ())), preferred_element_type=jnp.float32)


def exchange(values, axes):
    return lax.all_to_all(values, axes, split_axis=0, concat_axis=0, tiled=True)


def normalize(inputs, gain):
    values = inputs.astype(jnp.float32)
    scale = row_scale(values)
    unit = values * scale
    return scale, unit, (unit * gain).astype(jnp.bfloat16)


def body(
    teacher_input,
    expert_routes,
    route_gates,
    expert_gate_up,
    expert_down,
    student_owner,
    student_input,
    student_gain,
    align_weight,
):
    tok_rows, width_in = teacher_input.shape
    top_count = expert_routes.shape[1]
    size_x, size_z, size_y = (lax.axis_size(name) for name in DEV)
    owner_count = size_x * size_z * size_y
    plane_size = size_x * size_y
    plane = lax.axis_index("z")
    core = lax.axis_index("grp")
    capacity = 3 * tok_rows * top_count // (2 * owner_count)
    gate_up = expert_gate_up[0]
    down_proj = expert_down[0]
    width_out = down_proj.shape[1]
    half = width_out // 2
    shard_rows = align_weight.shape[0]
    width_student = student_input.shape[1]

    def halves(values):
        low, high = values[:, :half], values[:, half:]
        return jnp.where(core == 0, low, high), jnp.where(core == 0, high, low)

    gate_rows = route_gates.T
    coarse_rows = gate_rows.astype(jnp.bfloat16)
    fine_rows = (gate_rows - coarse_rows.astype(jnp.float32)).astype(jnp.bfloat16)
    owner_rows = jnp.broadcast_to(student_owner[None, :], (top_count, tok_rows))
    notes = jnp.concatenate(
        [
            expert_routes.T.astype(jnp.bfloat16),
            coarse_rows,
            fine_rows,
            owner_rows.astype(jnp.bfloat16),
        ],
        axis=1,
    )
    notes = jnp.pad(notes, ((0, 0), (0, width_in - notes.shape[1])))
    held = {0: jnp.concatenate([teacher_input, notes], axis=0)}
    for step in range(1, size_z // 2 + 1):
        held[step] = lax.ppermute(held[step - 1], "z", shifts(size_z, -1))
        if step > 1:
            held[1 - step] = lax.ppermute(held[2 - step], "z", shifts(size_z, 1))

    weight_kept = lax.all_gather(halves(align_weight)[0], DEV, axis=0, tiled=True)
    weight_given = lax.ppermute(weight_kept, "grp", SWAP)
    own_scale, own_unit, own_normed = normalize(student_input, student_gain)
    met_input = exchange(
        student_input.reshape(size_x, size_z, size_y, width_student)
        .transpose(0, 2, 1, 3)
        .reshape(plane_size, size_z, width_student),
        ("x", "y"),
    ).reshape(tok_rows, width_student)
    _, met_unit, met_normed = normalize(met_input, student_gain)
    met_xy = (
        met_normed.reshape(tok_rows, size_x, size_z, size_y, shard_rows)
        .transpose(0, 1, 3, 2, 4)
        .reshape(tok_rows, -1)
    )
    met_pair = jnp.concatenate([met_xy, lax.ppermute(met_xy, "grp", SWAP)], axis=0)
    forward = [
        dot_f32(normed, weight)
        for normed in (own_normed, met_normed)
        for weight in (weight_kept, weight_given)
    ]

    expert_ids = (
        jnp.arange(size_x)[:, None] * (size_z * size_y)
        + plane * size_y
        + jnp.arange(size_y)[None, :]
    ).reshape(-1)

    def places(group, base):
        routes, coarse, fine, owners = (
            jnp.concatenate(
                [
                    held[offset][tok_rows:, part * tok_rows : (part + 1) * tok_rows]
                    for offset in group
                ],
                axis=1,
            )
            for part in range(4)
        )
        named = routes.astype(jnp.int32)[None, :, :] == expert_ids[:, None, None]
        chosen = jnp.any(named, axis=1)
        at = jnp.arange(len(group) * tok_rows)
        before = (at[:, None] < at[None, :]) & (at[:, None] // tok_rows == at[None, :] // tok_rows)
        rank = dot_f32(chosen.astype(jnp.bfloat16), before.astype(jnp.bfloat16))
        first = (at // tok_rows * capacity + base + 1).astype(jnp.float32)
        spot = jnp.where(chosen, rank + first[None, :], 0.0)
        coarse = jnp.sum(jnp.where(named, coarse[None].astype(jnp.float32), 0.0), axis=1)
        fine = jnp.sum(jnp.where(named, fine[None].astype(jnp.float32), 0.0), axis=1)
        return spot, coarse, fine, owners[0].astype(jnp.int32)

    def numbers(base, count):
        return (base + 1 + jnp.arange(count)).astype(jnp.float32)[None, :, None]

    waiting = []
    arrived = None
    for parts in GROUPS:
        base = 0
        sent = []
        for group in parts:
            spot, coarse, fine, owner = places(group, base)
            slots = len(group) * capacity
            pick = (spot[:, None, :] == numbers(base, slots)).astype(jnp.bfloat16)
            feats = jnp.concatenate([held[offset][:tok_rows] for offset in group], axis=0)
            outgoing = dot_f32(pick.reshape(plane_size * slots, -1), feats).astype(jnp.bfloat16)
            if arrived is not None:
                outgoing, arrived = lax.optimization_barrier((outgoing, arrived))
                waiting[-1][-1][-1] = arrived
            arrived = exchange(outgoing.reshape(plane_size, slots, width_in), ("x", "y"))
            sent.append([spot, coarse, fine, owner, arrived])
            base += slots
            if len(sent) == 1:
                waiting.append(sent)
    produced = []
    for sent in waiting:
        rows = [
            expert_rows(one[-1].reshape(-1, width_in), gate_up, down_proj).reshape(
                plane_size, -1, width_out
            )
            for one in sent
        ]
        if sent is waiting[-2]:
            rows, last = lax.optimization_barrier((rows, waiting[-1][-1][-1]))
            waiting[-1][-1][-1] = last
        produced.append(jnp.concatenate(rows, axis=1))
    produced[-1], forward, met_pair = lax.optimization_barrier((produced[-1], forward, met_pair))
    own_kept, own_given, met_kept, met_given = forward

    teacher_out = jnp.zeros((tok_rows, width_out), jnp.float32)
    for group, sent, outgoing in zip(GROUPS, waiting, produced):
        offsets = [offset for part in group for offset in part]
        count = len(offsets)
        slots = count * capacity
        columns = count * tok_rows
        returned = exchange(outgoing, ("x", "y")).reshape(-1, width_out)
        spot, coarse, fine = (jnp.concatenate([one[n] for one in sent], axis=1) for n in range(3))
        owner = jnp.concatenate([one[3] for one in sent])
        ahead = (owner // size_y - plane) % size_z
        within = owner // (size_y * size_z) * size_y + owner % size_y
        at = jnp.arange(columns)
        goes = ahead * (count * plane_size) + at // tok_rows * plane_size + within
        moved = dot_f32(
            jnp.concatenate([spot, coarse, fine], axis=0).astype(jnp.bfloat16),
            one_hot(goes, columns),
        )
        spot, coarse, fine = jnp.split(moved, 3, axis=0)
        hot = spot[:, None, :] == numbers(0, slots)
        summed = sum(
            dot_t(
                jnp.where(hot, term[:, None, :], 0.0).astype(jnp.bfloat16).reshape(-1, columns),
                returned,
                (0,),
            )
            for term in (coarse, fine)
        ).astype(jnp.bfloat16)
        block = count * plane_size
        parts = [summed[:block]] + [
            lax.ppermute(summed[by * block : (by + 1) * block], "z", shifts(size_z, by))
            for by in range(1, size_z)
        ]
        apart = jnp.array([offset - by for by in range(size_z) for offset in offsets], jnp.int32)
        place = jnp.arange(plane_size)[None, :] * size_z + ((apart + plane) % size_z)[:, None]
        teacher_out = teacher_out + dot_t(
            one_hot(place.reshape(-1), tok_rows), jnp.concatenate(parts, axis=0), (0,)
        )
    teacher_target = (teacher_out * row_scale(teacher_out)).astype(jnp.bfloat16)

    target_kept, target_given = halves(teacher_target)
    met_kept = (met_kept - target_kept.astype(jnp.float32)).astype(jnp.bfloat16)
    met_given = (met_given - target_given.astype(jnp.float32)).astype(jnp.bfloat16)
    distance_pair = jnp.concatenate([met_kept, lax.ppermute(met_given, "grp", SWAP)], axis=0)
    term = dot_t(met_pair, distance_pair, (0,)).astype(jnp.bfloat16)
    met_grad = dot_t(met_kept, weight_kept, (1,)) + dot_t(met_given, weight_given, (1,))
    gain_part = jnp.sum(met_grad * met_unit, axis=0)
    gain_coarse = gain_part.astype(jnp.bfloat16)
    gain_fine = (gain_part - gain_coarse.astype(jnp.float32)).astype(jnp.bfloat16)
    gain_rows = -(-2 * width_student // (8 * half)) * 8
    gain_block = jnp.pad(
        jnp.concatenate([gain_coarse, gain_fine]), (0, gain_rows * half - 2 * width_student)
    ).reshape(1, gain_rows, half)
    term = jnp.concatenate(
        [
            term.reshape(plane_size, size_z * shard_rows, half),
            jnp.broadcast_to(gain_block, (plane_size, gain_rows, half)),
        ],
        axis=1,
    )
    relayed = exchange(teacher_target.reshape(plane_size, size_z, width_out), ("x", "y"))
    term = jnp.sum(exchange(term, ("x", "y")).astype(jnp.float32), axis=0)
    gain_block = term[size_z * shard_rows :].reshape(-1)[: 2 * width_student]
    gain_part = gain_block[:width_student] + gain_block[width_student:]
    term = term[: size_z * shard_rows].reshape(size_z, shard_rows, half)
    gain_rows = -(-width_student // half)
    gain_part = jnp.pad(gain_part, (0, gain_rows * half - width_student))
    gain_part = gain_part.reshape(1, gain_rows, half)
    term = jnp.concatenate(
        [term, jnp.broadcast_to(gain_part, (size_z, gain_rows, half))], axis=1
    )
    term = jnp.sum(exchange(term, "z"), axis=0)
    other = lax.ppermute(term, "grp", SWAP)
    grad_factor = 1.0 / math.sqrt(tok_rows * lax.axis_size("grp") * owner_count)
    gain_grad = (term + other)[shard_rows:].reshape(-1)[:width_student] * grad_factor
    term, other = term[:shard_rows] * grad_factor, other[:shard_rows] * grad_factor
    align_grad = jnp.where(
        core == 0,
        jnp.concatenate([term, other], axis=1),
        jnp.concatenate([other, term], axis=1),
    )

    student_target = (
        relayed.reshape(size_x, size_y, size_z, width_out)
        .transpose(0, 2, 1, 3)
        .reshape(tok_rows, width_out)
        .astype(jnp.float32)
    )
    target_kept, target_given = halves(student_target)
    own_kept, own_given = own_kept - target_kept, own_given - target_given
    token_loss = (
        jnp.sum(own_kept * own_kept, axis=-1) + jnp.sum(own_given * own_given, axis=-1)
    ) / width_out
    own_grad = dot_t(own_kept.astype(jnp.bfloat16), weight_kept, (1,)) + dot_t(
        own_given.astype(jnp.bfloat16), weight_given, (1,)
    )
    gain_inner = own_grad * student_gain
    input_grad = (
        own_scale
        * (gain_inner - own_unit * jnp.mean(gain_inner * own_unit, axis=-1, keepdims=True))
    ).astype(jnp.bfloat16)
    return (token_loss, input_grad, gain_grad, align_grad)


def solution(mesh):
    grid = Mesh(mesh.devices.reshape((mesh.devices.shape[0],) + DEV_SHAPE), ("grp",) + DEV)
    tokens = ("grp",) + DEV
    placed = (
        P(tokens, None),
        P(tokens, None),
        P(tokens, None),
        P(DEV, None, None),
        P(DEV, None, None),
        P(tokens),
        P(tokens, None),
        P(),
        P(DEV, None),
    )
    return jax.shard_map(
        body,
        mesh=grid,
        in_specs=placed,
        out_specs=(P(tokens), P(tokens, None), P(), P(DEV, None)),
        check_vma=False,
    )
```

```python
import math

import jax
import jax.numpy as jnp
from jax import lax
from jax.sharding import Mesh
from jax.sharding import PartitionSpec as P

epsilon = 1e-06
DEV = ("x", "z", "y")
DEV_SHAPE = (4, 8, 4)
SWAP = ((0, 1), (1, 0))
GROUPS = ((0, 1), (-1, 2, -2, 3), (-3, 4))
RETURNS = (2, 1, 0)


def shifts(count, by):
    return [(i, (i + by) % count) for i in range(count)]


def expert_rows(inputs, gate_up, down_proj):
    hidden_both = jnp.dot(inputs, gate_up, preferred_element_type=jnp.float32)
    split_at = gate_up.shape[1] // 2
    hidden = (jax.nn.silu(hidden_both[:, :split_at]) * hidden_both[:, split_at:]).astype(
        jnp.bfloat16
    )
    return jnp.dot(hidden, down_proj, preferred_element_type=jnp.float32).astype(jnp.bfloat16)


def row_scale(values):
    return lax.rsqrt(jnp.mean(values * values, axis=-1, keepdims=True) + epsilon)


def one_hot(index, count):
    return (index[:, None] == jnp.arange(count, dtype=index.dtype)[None, :]).astype(jnp.bfloat16)


def dot_f32(left, right):
    return jnp.dot(left, right, preferred_element_type=jnp.float32)


def dot_t(left, right, dims):
    return lax.dot_general(left, right, ((dims, dims), ((), ())), preferred_element_type=jnp.float32)


def exchange(values, axes):
    return lax.all_to_all(values, axes, split_axis=0, concat_axis=0, tiled=True)


def normalize(inputs, gain):
    values = inputs.astype(jnp.float32)
    scale = row_scale(values)
    unit = values * scale
    return scale, unit, (unit * gain).astype(jnp.bfloat16)


def body(
    teacher_input,
    expert_routes,
    route_gates,
    expert_gate_up,
    expert_down,
    student_owner,
    student_input,
    student_gain,
    align_weight,
):
    tok_rows, width_in = teacher_input.shape
    top_count = expert_routes.shape[1]
    size_x, size_z, size_y = (lax.axis_size(name) for name in DEV)
    owner_count = size_x * size_z * size_y
    plane_size = size_x * size_y
    plane = lax.axis_index("z")
    core = lax.axis_index("grp")
    capacity = 3 * tok_rows * top_count // (2 * owner_count)
    gate_up = expert_gate_up[0]
    down_proj = expert_down[0]
    width_out = down_proj.shape[1]
    half = width_out // 2
    shard_rows = align_weight.shape[0]
    width_student = student_input.shape[1]

    def halves(values):
        low, high = values[:, :half], values[:, half:]
        return jnp.where(core == 0, low, high), jnp.where(core == 0, high, low)

    gate_rows = route_gates.T
    coarse_rows = gate_rows.astype(jnp.bfloat16)
    fine_rows = (gate_rows - coarse_rows.astype(jnp.float32)).astype(jnp.bfloat16)
    weight_rows = halves(align_weight)[0].reshape(top_count, -1)
    notes = jnp.concatenate(
        [expert_routes.T.astype(jnp.bfloat16), coarse_rows, fine_rows, weight_rows], axis=1
    )
    notes_end = notes.shape[1]
    notes = jnp.pad(notes, ((0, 0), (0, width_in - notes.shape[1])))
    held = {0: jnp.concatenate([teacher_input, notes], axis=0)}

    def ring(step):
        held[step] = lax.ppermute(held[step - 1], "z", shifts(size_z, -1))
        if step > 1:
            held[1 - step] = lax.ppermute(held[2 - step], "z", shifts(size_z, 1))

    ring(1)
    def by_axes(values):
        lead = values.shape[:-1]
        values = values.reshape(*lead, size_x, size_z, size_y, shard_rows)
        return jnp.swapaxes(values, -3, -2).reshape(*lead, -1)

    def by_shards(values):
        lead = values.shape[:-1]
        values = values.reshape(*lead, size_x, size_y, size_z, shard_rows)
        return jnp.swapaxes(values, -3, -2).reshape(*lead, -1)

    expert_ids = (
        jnp.arange(size_x)[:, None] * (size_z * size_y)
        + plane * size_y
        + jnp.arange(size_y)[None, :]
    ).reshape(-1)

    def places(group):
        routes, coarse, fine = (
            jnp.concatenate(
                [
                    held[offset][tok_rows:, part * tok_rows : (part + 1) * tok_rows]
                    for offset in group
                ],
                axis=1,
            )
            for part in range(3)
        )
        named = routes.astype(jnp.int32)[None, :, :] == expert_ids[:, None, None]
        chosen = jnp.any(named, axis=1)
        at = jnp.arange(len(group) * tok_rows)
        before = (at[:, None] < at[None, :]) & (at[:, None] // tok_rows == at[None, :] // tok_rows)
        rank = dot_f32(chosen.astype(jnp.bfloat16), before.astype(jnp.bfloat16))
        first = (at // tok_rows * capacity + 1).astype(jnp.float32)
        spot = jnp.where(chosen, rank + first[None, :], 0.0)
        coarse = jnp.sum(jnp.where(named, coarse[None].astype(jnp.float32), 0.0), axis=1)
        fine = jnp.sum(jnp.where(named, fine[None].astype(jnp.float32), 0.0), axis=1)
        numbers = jnp.arange(1, len(group) * capacity + 1).astype(jnp.float32)
        return spot[:, None, :] == numbers[None, :, None], coarse, fine

    def gated(group, spots, returned):
        hot, coarse, fine = spots
        returned = returned.reshape(-1, width_out)
        summed = sum(
            dot_t(
                jnp.where(hot, term[:, None, :], 0.0)
                .astype(jnp.bfloat16)
                .reshape(returned.shape[0], -1),
                returned,
                (0,),
            )
            for term in (coarse, fine)
        )
        total = 0.0
        for n, offset in enumerate(group):
            part = summed[n * tok_rows : (n + 1) * tok_rows]
            if offset:
                part = lax.ppermute(part.astype(jnp.bfloat16), "z", shifts(size_z, offset))
            total = total + part.astype(jnp.float32)
        return total

    placed, arrived = [], []
    for group in GROUPS:
        hot, coarse, fine = places(group)
        placed.append((hot, coarse, fine))
        feats = jnp.concatenate([held[offset][:tok_rows] for offset in group], axis=0)
        pick = hot.astype(jnp.bfloat16).reshape(-1, feats.shape[0])
        outgoing = dot_f32(pick, feats).astype(jnp.bfloat16)
        if arrived:
            outgoing, arrived[-1] = lax.optimization_barrier((outgoing, arrived[-1]))
        else:
            outgoing, held[1], held[0] = lax.optimization_barrier((outgoing, held[1], held[0]))
            for step in range(2, size_z // 2 + 1):
                ring(step)
        arrived.append(exchange(outgoing.reshape(plane_size, -1, width_in), ("x", "y")))
    weight_kept = jnp.zeros((size_z,) + weight_rows.shape, weight_rows.dtype)
    for u in range(size_z):
        rows = held[u if u in held else u - size_z][tok_rows:, :notes_end]
        weight_kept = lax.dynamic_update_index_in_dim(
            weight_kept, rows[:, notes_end - weight_rows.shape[1] :], (plane + u) % size_z, axis=0
        )
    weight_kept = weight_kept.reshape(size_z * shard_rows, half)
    weight_kept = lax.all_gather(weight_kept, ("x", "y"), axis=0, tiled=True)
    weight_given = lax.ppermute(weight_kept, "grp", SWAP)

    produced = [
        expert_rows(rows.reshape(-1, width_in), gate_up, down_proj) for rows in arrived[:-1]
    ]
    arrived[-1], produced = lax.optimization_barrier((arrived[-1], produced))
    produced.append(expert_rows(arrived[-1].reshape(-1, width_in), gate_up, down_proj))
    teacher_out = jnp.zeros((tok_rows, width_out), jnp.float32)
    outgoing = produced[RETURNS[0]]
    for number, turn in enumerate(RETURNS):
        returned = exchange(outgoing.reshape(plane_size, -1, width_out), ("x", "y"))
        if turn != RETURNS[-1]:
            outgoing, returned = lax.optimization_barrier((produced[RETURNS[number + 1]], returned))
        teacher_out = teacher_out + gated(GROUPS[turn], placed[turn], returned)
    gain_axes = by_axes(student_gain)
    scale_rows, unit_rows, normed = normalize(by_axes(student_input), gain_axes)
    normed_pair = jnp.concatenate([normed, lax.ppermute(normed, "grp", SWAP)], axis=0)
    forward = [dot_f32(normed, weight) for weight in (weight_kept, weight_given)]

    teacher_target = (teacher_out * row_scale(teacher_out)).astype(jnp.bfloat16)

    relay = dot_t(one_hot(student_owner, owner_count), teacher_target, (0,)).astype(jnp.bfloat16)
    relay = exchange(relay.reshape(owner_count, -1, width_out // 2), DEV)
    target_kept, target_given = halves(relay.reshape(tok_rows, width_out).astype(jnp.float32))
    own_kept, own_given = forward[0] - target_kept, forward[1] - target_given
    kept_bf, given_bf = own_kept.astype(jnp.bfloat16), own_given.astype(jnp.bfloat16)
    distance_pair = jnp.concatenate([kept_bf, lax.ppermute(given_bf, "grp", SWAP)], axis=0)
    term = dot_t(normed_pair, distance_pair, (0,)).astype(jnp.bfloat16)
    normed_grad = dot_t(kept_bf, weight_kept, (1,)) + dot_t(given_bf, weight_given, (1,))
    gain_part = jnp.sum(normed_grad * unit_rows, axis=0)
    gain_coarse = gain_part.astype(jnp.bfloat16)
    gain_fine = (gain_part - gain_coarse.astype(jnp.float32)).astype(jnp.bfloat16)
    gain_rows = -(-2 * width_student // (8 * half)) * 8
    gain_block = jnp.pad(
        jnp.concatenate([gain_coarse, gain_fine]), (0, gain_rows * half - 2 * width_student)
    ).reshape(1, gain_rows, half)
    term = jnp.concatenate(
        [
            term.reshape(plane_size, size_z * shard_rows, half),
            jnp.broadcast_to(gain_block, (plane_size, gain_rows, half)),
        ],
        axis=1,
    )
    term = jnp.sum(exchange(term, ("x", "y")).astype(jnp.float32), axis=0)
    gain_block = term[size_z * shard_rows :].reshape(-1)[: 2 * width_student]
    gain_part = gain_block[:width_student] + gain_block[width_student:]
    term = term[: size_z * shard_rows].reshape(size_z, shard_rows, half)
    gain_rows = -(-width_student // half)
    gain_part = jnp.pad(gain_part, (0, gain_rows * half - width_student))
    gain_part = gain_part.reshape(1, gain_rows, half)
    term = jnp.concatenate(
        [term, jnp.broadcast_to(gain_part, (size_z, gain_rows, half))], axis=1
    )
    term = jnp.sum(exchange(term, "z"), axis=0)
    other = lax.ppermute(term, "grp", SWAP)
    grad_factor = 1.0 / math.sqrt(tok_rows * lax.axis_size("grp") * owner_count)
    gain_grad = by_shards((term + other)[shard_rows:].reshape(-1)[:width_student]) * grad_factor
    term, other = term[:shard_rows] * grad_factor, other[:shard_rows] * grad_factor
    align_grad = jnp.where(
        core == 0,
        jnp.concatenate([term, other], axis=1),
        jnp.concatenate([other, term], axis=1),
    )

    token_loss = (
        jnp.sum(own_kept * own_kept, axis=-1) + jnp.sum(own_given * own_given, axis=-1)
    ) / width_out
    gain_inner = normed_grad * gain_axes
    input_grad = by_shards(
        (
            scale_rows
            * (gain_inner - unit_rows * jnp.mean(gain_inner * unit_rows, axis=-1, keepdims=True))
        ).astype(jnp.bfloat16)
    )
    return (token_loss, input_grad, gain_grad, align_grad)


def solution(mesh):
    grid = Mesh(mesh.devices.reshape((mesh.devices.shape[0],) + DEV_SHAPE), ("grp",) + DEV)
    tokens = ("grp",) + DEV
    placed = (
        P(tokens, None),
        P(tokens, None),
        P(tokens, None),
        P(DEV, None, None),
        P(DEV, None, None),
        P(tokens),
        P(tokens, None),
        P(),
        P(DEV, None),
    )
    return jax.shard_map(
        body,
        mesh=grid,
        in_specs=placed,
        out_specs=(P(tokens), P(tokens, None), P(), P(DEV, None)),
        check_vma=False,
    )
```

```python
import math

import jax
import jax.numpy as jnp
from jax import lax
from jax.sharding import Mesh
from jax.sharding import PartitionSpec as P

epsilon = 1e-06
DEV = ("x", "z", "y")
DEV_SHAPE = (4, 8, 4)
SWAP = ((0, 1), (1, 0))
GROUPS = ((0, 1), (-1, 2), (-2, 3, -3, 4))
RETURNS = ((2,), (0, 1))


def shifts(count, by):
    return [(i, (i + by) % count) for i in range(count)]


def expert_rows(inputs, gate_up, down_proj):
    hidden_both = jnp.dot(inputs, gate_up, preferred_element_type=jnp.float32)
    split_at = gate_up.shape[1] // 2
    hidden = (jax.nn.silu(hidden_both[:, :split_at]) * hidden_both[:, split_at:]).astype(
        jnp.bfloat16
    )
    return jnp.dot(hidden, down_proj, preferred_element_type=jnp.float32).astype(jnp.bfloat16)


def row_scale(values):
    return lax.rsqrt(jnp.mean(values * values, axis=-1, keepdims=True) + epsilon)


def one_hot(index, count):
    return (index[:, None] == jnp.arange(count, dtype=index.dtype)[None, :]).astype(jnp.bfloat16)


def dot_f32(left, right):
    return jnp.dot(left, right, preferred_element_type=jnp.float32)


def dot_t(left, right, dims):
    return lax.dot_general(left, right, ((dims, dims), ((), ())), preferred_element_type=jnp.float32)


def exchange(values, axes):
    return lax.all_to_all(values, axes, split_axis=0, concat_axis=0, tiled=True)


def normalize(inputs, gain):
    values = inputs.astype(jnp.float32)
    scale = row_scale(values)
    unit = values * scale
    return scale, unit, (unit * gain).astype(jnp.bfloat16)


def body(
    teacher_input,
    expert_routes,
    route_gates,
    expert_gate_up,
    expert_down,
    student_owner,
    student_input,
    student_gain,
    align_weight,
):
    tok_rows, width_in = teacher_input.shape
    top_count = expert_routes.shape[1]
    size_x, size_z, size_y = (lax.axis_size(name) for name in DEV)
    owner_count = size_x * size_z * size_y
    plane_size = size_x * size_y
    plane = lax.axis_index("z")
    core = lax.axis_index("grp")
    capacity = 3 * tok_rows * top_count // (2 * owner_count)
    gate_up = expert_gate_up[0]
    down_proj = expert_down[0]
    width_out = down_proj.shape[1]
    half = width_out // 2
    shard_rows = align_weight.shape[0]
    width_student = student_input.shape[1]

    def halves(values):
        low, high = values[:, :half], values[:, half:]
        return jnp.where(core == 0, low, high), jnp.where(core == 0, high, low)

    gate_rows = route_gates.T
    coarse_rows = gate_rows.astype(jnp.bfloat16)
    fine_rows = (gate_rows - coarse_rows.astype(jnp.float32)).astype(jnp.bfloat16)
    notes = jnp.concatenate(
        [expert_routes.T.astype(jnp.bfloat16), coarse_rows, fine_rows], axis=1
    )
    weight_rows = align_weight.reshape(top_count, -1)
    notes = jnp.concatenate(
        [
            jnp.pad(rows, ((0, 0), (0, width_in - rows.shape[1])))
            for rows in (notes, weight_rows)
        ],
        axis=0,
    )
    held = {0: jnp.concatenate([teacher_input, notes], axis=0)}

    def ring(step):
        held[step] = lax.ppermute(held[step - 1], "z", shifts(size_z, -1))
        if step > 1:
            held[1 - step] = lax.ppermute(held[2 - step], "z", shifts(size_z, 1))

    ring(1)
    def by_axes(values):
        lead = values.shape[:-1]
        values = values.reshape(*lead, size_x, size_z, size_y, shard_rows)
        return jnp.swapaxes(values, -3, -2).reshape(*lead, -1)

    def by_shards(values):
        lead = values.shape[:-1]
        values = values.reshape(*lead, size_x, size_y, size_z, shard_rows)
        return jnp.swapaxes(values, -3, -2).reshape(*lead, -1)

    expert_ids = (
        jnp.arange(size_x)[:, None] * (size_z * size_y)
        + plane * size_y
        + jnp.arange(size_y)[None, :]
    ).reshape(-1)

    def places(group):
        routes, coarse, fine = (
            jnp.concatenate(
                [
                    held[offset][tok_rows:-top_count, part * tok_rows : (part + 1) * tok_rows]
                    for offset in group
                ],
                axis=1,
            )
            for part in range(3)
        )
        named = routes.astype(jnp.int32)[None, :, :] == expert_ids[:, None, None]
        chosen = jnp.any(named, axis=1)
        at = jnp.arange(len(group) * tok_rows)
        before = (at[:, None] < at[None, :]) & (at[:, None] // tok_rows == at[None, :] // tok_rows)
        rank = dot_f32(chosen.astype(jnp.bfloat16), before.astype(jnp.bfloat16))
        first = (at // tok_rows * capacity + 1).astype(jnp.float32)
        spot = jnp.where(chosen, rank + first[None, :], 0.0)
        coarse = jnp.sum(jnp.where(named, coarse[None].astype(jnp.float32), 0.0), axis=1)
        fine = jnp.sum(jnp.where(named, fine[None].astype(jnp.float32), 0.0), axis=1)
        numbers = jnp.arange(1, len(group) * capacity + 1).astype(jnp.float32)
        return spot[:, None, :] == numbers[None, :, None], coarse, fine

    def gated(numbers, returned):
        offsets = [offset for number in numbers for offset in GROUPS[number]]
        slots = [placed[number][0].shape[1] for number in numbers]
        hot = jnp.concatenate(
            [
                jnp.pad(
                    placed[number][0],
                    ((0, 0), (sum(slots[:n]), sum(slots[n + 1 :])), (0, 0)),
                )
                for n, number in enumerate(numbers)
            ],
            axis=2,
        )
        returned = returned.reshape(-1, width_out)
        summed = sum(
            dot_t(
                jnp.where(
                    hot,
                    jnp.concatenate([placed[number][term] for number in numbers], axis=1)[:, None],
                    0.0,
                )
                .astype(jnp.bfloat16)
                .reshape(returned.shape[0], -1),
                returned,
                (0,),
            )
            for term in (1, 2)
        )
        part = {
            offset: summed[n * tok_rows : (n + 1) * tok_rows] for n, offset in enumerate(offsets)
        }

        return part

    def moved(values, by):
        if not by:
            return values
        return lax.ppermute(values.astype(jnp.bfloat16), "z", shifts(size_z, by)).astype(
            jnp.float32
        )

    placed, arrived = [], []
    for group in GROUPS:
        hot, coarse, fine = places(group)
        placed.append((hot, coarse, fine))
        feats = jnp.concatenate([held[offset][:tok_rows] for offset in group], axis=0)
        pick = hot.astype(jnp.bfloat16).reshape(-1, feats.shape[0])
        outgoing = dot_f32(pick, feats).astype(jnp.bfloat16)
        if arrived:
            outgoing, arrived[-1] = lax.optimization_barrier((outgoing, arrived[-1]))
        else:
            outgoing, held[1], held[0] = lax.optimization_barrier((outgoing, held[1], held[0]))
            for step in range(2, size_z // 2 + 1):
                ring(step)
        arrived.append(exchange(outgoing.reshape(plane_size, -1, width_in), ("x", "y")))
    full_weight = jnp.zeros((size_z,) + weight_rows.shape, weight_rows.dtype)
    for u in range(size_z):
        rows = held[u if u in held else u - size_z][-top_count:, : weight_rows.shape[1]]
        full_weight = lax.dynamic_update_index_in_dim(
            full_weight, rows, (plane + u) % size_z, axis=0
        )
    full_weight = full_weight.reshape(size_z * shard_rows, width_out)

    produced = [
        expert_rows(rows.reshape(-1, width_in), gate_up, down_proj) for rows in arrived[:-1]
    ]
    arrived[-1], produced = lax.optimization_barrier((arrived[-1], produced))
    produced.append(expert_rows(arrived[-1].reshape(-1, width_in), gate_up, down_proj))
    produced = [rows.reshape(plane_size, -1, width_out) for rows in produced]
    far, near = RETURNS
    returned = exchange(jnp.concatenate([produced[n] for n in far], axis=1), ("x", "y"))
    outgoing, returned, full_weight = lax.optimization_barrier(
        (jnp.concatenate([produced[n] for n in near], axis=1), returned, full_weight)
    )
    full_weight = lax.all_gather(full_weight, ("x", "y"), axis=0, tiled=True)
    back = gated(far, returned)
    returned = exchange(outgoing, ("x", "y"))
    ahead = moved(back[3] + moved(back[4], 1), 1)
    behind = moved(back[-2] + moved(back[-3], -1), -1)
    returned, ahead, behind = lax.optimization_barrier((returned, ahead, behind))
    back = gated(near, returned)
    teacher_out = (
        back[0]
        + moved(back[-1] + behind, -1)
        + moved(back[2] + ahead, 2)
        + moved(back[1], 1)
    )
    teacher_target = (teacher_out * row_scale(teacher_out)).astype(jnp.bfloat16)

    relay = dot_t(one_hot(student_owner, owner_count), teacher_target, (0,)).astype(jnp.bfloat16)
    relay, student_input = lax.optimization_barrier((relay, student_input))
    relay = exchange(relay.reshape(owner_count, -1, width_out // 2), DEV)
    gain_axes = by_axes(student_gain)
    scale_rows, unit_rows, normed = normalize(by_axes(student_input), gain_axes)
    normed_pair = jnp.concatenate([normed, lax.ppermute(normed, "grp", SWAP)], axis=0)
    student_out = dot_f32(normed, full_weight)

    distance = student_out - relay.reshape(tok_rows, width_out).astype(jnp.float32)
    distance_bf = distance.astype(jnp.bfloat16)
    kept, given = halves(distance_bf)
    distance_pair = jnp.concatenate([kept, lax.ppermute(given, "grp", SWAP)], axis=0)
    term = dot_t(normed_pair, distance_pair, (0,)).astype(jnp.bfloat16)
    normed_grad = dot_t(distance_bf, full_weight, (1,))
    gain_part = jnp.sum(normed_grad * unit_rows, axis=0)
    gain_coarse = gain_part.astype(jnp.bfloat16)
    gain_fine = (gain_part - gain_coarse.astype(jnp.float32)).astype(jnp.bfloat16)
    gain_rows = -(-2 * width_student // (8 * half)) * 8
    gain_block = jnp.pad(
        jnp.concatenate([gain_coarse, gain_fine]), (0, gain_rows * half - 2 * width_student)
    ).reshape(1, gain_rows, half)
    term = jnp.concatenate(
        [
            term.reshape(plane_size, size_z * shard_rows, half),
            jnp.broadcast_to(gain_block, (plane_size, gain_rows, half)),
        ],
        axis=1,
    )
    term = jnp.sum(exchange(term, ("x", "y")).astype(jnp.float32), axis=0)
    gain_block = term[size_z * shard_rows :].reshape(-1)[: 2 * width_student]
    gain_part = gain_block[:width_student] + gain_block[width_student:]
    term = term[: size_z * shard_rows].reshape(size_z, shard_rows, half)
    gain_rows = -(-width_student // half)
    gain_part = jnp.pad(gain_part, (0, gain_rows * half - width_student))
    gain_part = gain_part.reshape(1, gain_rows, half)
    term = jnp.concatenate(
        [term, jnp.broadcast_to(gain_part, (size_z, gain_rows, half))], axis=1
    )
    term = jnp.sum(exchange(term, "z"), axis=0)
    other = lax.ppermute(term, "grp", SWAP)
    grad_factor = 1.0 / math.sqrt(tok_rows * lax.axis_size("grp") * owner_count)
    gain_grad = by_shards((term + other)[shard_rows:].reshape(-1)[:width_student]) * grad_factor
    term, other = term[:shard_rows] * grad_factor, other[:shard_rows] * grad_factor
    align_grad = jnp.where(
        core == 0,
        jnp.concatenate([term, other], axis=1),
        jnp.concatenate([other, term], axis=1),
    )

    token_loss = jnp.mean(distance * distance, axis=-1)
    gain_inner = normed_grad * gain_axes
    input_grad = by_shards(
        (
            scale_rows
            * (gain_inner - unit_rows * jnp.mean(gain_inner * unit_rows, axis=-1, keepdims=True))
        ).astype(jnp.bfloat16)
    )
    return (token_loss, input_grad, gain_grad, align_grad)


def solution(mesh):
    grid = Mesh(mesh.devices.reshape((mesh.devices.shape[0],) + DEV_SHAPE), ("grp",) + DEV)
    tokens = ("grp",) + DEV
    placed = (
        P(tokens, None),
        P(tokens, None),
        P(tokens, None),
        P(DEV, None, None),
        P(DEV, None, None),
        P(tokens),
        P(tokens, None),
        P(),
        P(DEV, None),
    )
    return jax.shard_map(
        body,
        mesh=grid,
        in_specs=placed,
        out_specs=(P(tokens), P(tokens, None), P(), P(DEV, None)),
        check_vma=False,
    )
```

```python
import math

import jax
import jax.numpy as jnp
from jax import lax
from jax.sharding import Mesh
from jax.sharding import PartitionSpec as P

epsilon = 1e-06
DEV = ("x", "z", "y")
DEV_SHAPE = (4, 8, 4)
SWAP = ((0, 1), (1, 0))
GROUPS = ((0, 1), (-1, 2), (-2, 3, -3, 4))
RETURNS = ((0, 1), (2,))


def shifts(count, by):
    return [(i, (i + by) % count) for i in range(count)]


def expert_rows(inputs, gate_up, down_proj):
    hidden_both = jnp.dot(inputs, gate_up, preferred_element_type=jnp.float32)
    split_at = gate_up.shape[1] // 2
    hidden = (jax.nn.silu(hidden_both[:, :split_at]) * hidden_both[:, split_at:]).astype(
        jnp.bfloat16
    )
    return jnp.dot(hidden, down_proj, preferred_element_type=jnp.float32).astype(jnp.bfloat16)


def row_scale(values):
    return lax.rsqrt(jnp.mean(values * values, axis=-1, keepdims=True) + epsilon)


def one_hot(index, count):
    return (index[:, None] == jnp.arange(count, dtype=index.dtype)[None, :]).astype(jnp.bfloat16)


def dot_f32(left, right):
    return jnp.dot(left, right, preferred_element_type=jnp.float32)


def dot_t(left, right, dims):
    return lax.dot_general(left, right, ((dims, dims), ((), ())), preferred_element_type=jnp.float32)


def exchange(values, axes):
    return lax.all_to_all(values, axes, split_axis=0, concat_axis=0, tiled=True)


def normalize(inputs, gain):
    values = inputs.astype(jnp.float32)
    scale = row_scale(values)
    unit = values * scale
    return scale, unit, (unit * gain).astype(jnp.bfloat16)


def body(
    teacher_input,
    expert_routes,
    route_gates,
    expert_gate_up,
    expert_down,
    student_owner,
    student_input,
    student_gain,
    align_weight,
):
    tok_rows, width_in = teacher_input.shape
    top_count = expert_routes.shape[1]
    size_x, size_z, size_y = (lax.axis_size(name) for name in DEV)
    owner_count = size_x * size_z * size_y
    plane_size = size_x * size_y
    plane = lax.axis_index("z")
    core = lax.axis_index("grp")
    capacity = 3 * tok_rows * top_count // (2 * owner_count)
    gate_up = expert_gate_up[0]
    down_proj = expert_down[0]
    width_out = down_proj.shape[1]
    half = width_out // 2
    shard_rows = align_weight.shape[0]
    width_student = student_input.shape[1]

    def halves(values):
        low, high = values[:, :half], values[:, half:]
        return jnp.where(core == 0, low, high), jnp.where(core == 0, high, low)

    gate_rows = route_gates.T
    coarse_rows = gate_rows.astype(jnp.bfloat16)
    fine_rows = (gate_rows - coarse_rows.astype(jnp.float32)).astype(jnp.bfloat16)
    notes = jnp.concatenate(
        [expert_routes.T.astype(jnp.bfloat16), coarse_rows, fine_rows], axis=1
    )
    weight_rows = align_weight.reshape(top_count, -1)
    notes = jnp.concatenate(
        [
            jnp.pad(rows, ((0, 0), (0, width_in - rows.shape[1])))
            for rows in (notes, weight_rows)
        ],
        axis=0,
    )
    held = {0: jnp.concatenate([teacher_input, notes], axis=0)}

    def ring(step):
        held[step] = lax.ppermute(held[step - 1], "z", shifts(size_z, -1))
        if step > 1:
            held[1 - step] = lax.ppermute(held[2 - step], "z", shifts(size_z, 1))

    ring(1)
    def by_axes(values):
        lead = values.shape[:-1]
        values = values.reshape(*lead, size_x, size_z, size_y, shard_rows)
        return jnp.swapaxes(values, -3, -2).reshape(*lead, -1)

    def by_shards(values):
        lead = values.shape[:-1]
        values = values.reshape(*lead, size_x, size_y, size_z, shard_rows)
        return jnp.swapaxes(values, -3, -2).reshape(*lead, -1)

    expert_ids = (
        jnp.arange(size_x)[:, None] * (size_z * size_y)
        + plane * size_y
        + jnp.arange(size_y)[None, :]
    ).reshape(-1)

    def places(group):
        routes, coarse, fine = (
            jnp.concatenate(
                [
                    held[offset][tok_rows:-top_count, part * tok_rows : (part + 1) * tok_rows]
                    for offset in group
                ],
                axis=1,
            )
            for part in range(3)
        )
        named = routes.astype(jnp.int32)[None, :, :] == expert_ids[:, None, None]
        chosen = jnp.any(named, axis=1)
        at = jnp.arange(len(group) * tok_rows)
        before = (at[:, None] < at[None, :]) & (at[:, None] // tok_rows == at[None, :] // tok_rows)
        rank = dot_f32(chosen.astype(jnp.bfloat16), before.astype(jnp.bfloat16))
        first = (at // tok_rows * capacity + 1).astype(jnp.float32)
        spot = jnp.where(chosen, rank + first[None, :], 0.0)
        coarse = jnp.sum(jnp.where(named, coarse[None].astype(jnp.float32), 0.0), axis=1)
        fine = jnp.sum(jnp.where(named, fine[None].astype(jnp.float32), 0.0), axis=1)
        numbers = jnp.arange(1, len(group) * capacity + 1).astype(jnp.float32)
        wide = jnp.pad(
            spot.reshape(plane_size, len(group), tok_rows),
            ((0, 0), (0, 0), (0, held[0].shape[0] - tok_rows)),
        ).reshape(plane_size, -1)
        hot, pick = (where[:, None, :] == numbers[None, :, None] for where in (spot, wide))
        return hot, coarse, fine, pick

    def gated(numbers, returned):
        offsets = [offset for number in numbers for offset in GROUPS[number]]
        slots = [placed[number][0].shape[1] for number in numbers]
        hot = jnp.concatenate(
            [
                jnp.pad(
                    placed[number][0],
                    ((0, 0), (sum(slots[:n]), sum(slots[n + 1 :])), (0, 0)),
                )
                for n, number in enumerate(numbers)
            ],
            axis=2,
        )
        returned = returned.reshape(-1, width_out)
        summed = sum(
            dot_t(
                jnp.where(
                    hot,
                    jnp.concatenate([placed[number][term] for number in numbers], axis=1)[:, None],
                    0.0,
                )
                .astype(jnp.bfloat16)
                .reshape(returned.shape[0], -1),
                returned,
                (0,),
            )
            for term in (1, 2)
        )
        part = {
            offset: summed[n * tok_rows : (n + 1) * tok_rows] for n, offset in enumerate(offsets)
        }

        return part

    def moved(values, by):
        if not by:
            return values
        return lax.ppermute(values.astype(jnp.bfloat16), "z", shifts(size_z, by)).astype(
            jnp.float32
        )

    placed, arrived = [], []
    for group in GROUPS:
        hot, coarse, fine, pick = places(group)
        placed.append((hot, coarse, fine))
        feats = jnp.concatenate([held[offset] for offset in group], axis=0)
        pick = pick.astype(jnp.bfloat16).reshape(-1, feats.shape[0])
        outgoing = dot_f32(pick, feats).astype(jnp.bfloat16)
        if arrived:
            outgoing, arrived[-1] = lax.optimization_barrier((outgoing, arrived[-1]))
        else:
            outgoing, held[1], held[0] = lax.optimization_barrier((outgoing, held[1], held[0]))
            for step in range(2, size_z // 2 + 1):
                ring(step)
        arrived.append(exchange(outgoing.reshape(plane_size, -1, width_in), ("x", "y")))
    full_weight = jnp.zeros((size_z,) + weight_rows.shape, weight_rows.dtype)
    for u in range(size_z):
        rows = held[u if u in held else u - size_z][-top_count:, : weight_rows.shape[1]]
        full_weight = lax.dynamic_update_index_in_dim(
            full_weight, rows, (plane + u) % size_z, axis=0
        )
    full_weight = full_weight.reshape(size_z * shard_rows, width_out)

    produced = [
        expert_rows(rows.reshape(-1, width_in), gate_up, down_proj) for rows in arrived[:-1]
    ]
    arrived[-1], produced = lax.optimization_barrier((arrived[-1], produced))
    produced.append(expert_rows(arrived[-1].reshape(-1, width_in), gate_up, down_proj))
    produced = [rows.reshape(plane_size, -1, width_out) for rows in produced]
    near, far = RETURNS
    returned = exchange(jnp.concatenate([produced[n] for n in near], axis=1), ("x", "y"))
    outgoing, returned, full_weight = lax.optimization_barrier(
        (jnp.concatenate([produced[n] for n in far], axis=1), returned, full_weight)
    )
    full_weight = lax.all_gather(full_weight, ("x", "y"), axis=0, tiled=True)
    back = gated(near, returned)
    teacher_out = sum(moved(back[offset], offset) for offset in (2, -1, 1, 0))
    returned = exchange(outgoing, ("x", "y"))
    back = gated(far, returned)
    ahead, behind, teacher_out = lax.optimization_barrier(
        (back[3] + moved(back[4], 1), back[-2] + moved(back[-3], -1), teacher_out)
    )
    teacher_out = teacher_out + moved(ahead, 3) + moved(behind, -2)
    teacher_target = (teacher_out * row_scale(teacher_out)).astype(jnp.bfloat16)

    relay = dot_t(one_hot(student_owner, owner_count), teacher_target, (0,)).astype(jnp.bfloat16)
    relay, student_input = lax.optimization_barrier((relay, student_input))
    relay = exchange(relay.reshape(owner_count, -1, width_out // 2), DEV)
    gain_axes = by_axes(student_gain)
    scale_rows, unit_rows, normed = normalize(by_axes(student_input), gain_axes)
    normed_pair = jnp.concatenate([normed, lax.ppermute(normed, "grp", SWAP)], axis=0)
    student_out = dot_f32(normed, full_weight)

    distance = student_out - relay.reshape(tok_rows, width_out).astype(jnp.float32)
    distance_bf = distance.astype(jnp.bfloat16)
    kept, given = halves(distance_bf)
    distance_pair = jnp.concatenate([kept, lax.ppermute(given, "grp", SWAP)], axis=0)
    term = dot_t(normed_pair, distance_pair, (0,)).astype(jnp.bfloat16)
    normed_grad = dot_t(distance_bf, full_weight, (1,))
    gain_part = jnp.sum(normed_grad * unit_rows, axis=0)
    gain_coarse = gain_part.astype(jnp.bfloat16)
    gain_fine = (gain_part - gain_coarse.astype(jnp.float32)).astype(jnp.bfloat16)
    gain_rows = -(-2 * width_student // (8 * half)) * 8
    gain_block = jnp.pad(
        jnp.concatenate([gain_coarse, gain_fine]), (0, gain_rows * half - 2 * width_student)
    ).reshape(1, gain_rows, half)
    term = jnp.concatenate(
        [
            term.reshape(plane_size, size_z * shard_rows, half),
            jnp.broadcast_to(gain_block, (plane_size, gain_rows, half)),
        ],
        axis=1,
    )
    term = jnp.sum(exchange(term, ("x", "y")).astype(jnp.float32), axis=0)
    gain_block = term[size_z * shard_rows :].reshape(-1)[: 2 * width_student]
    gain_part = gain_block[:width_student] + gain_block[width_student:]
    term = term[: size_z * shard_rows].reshape(size_z, shard_rows, half)
    gain_rows = -(-width_student // half)
    gain_part = jnp.pad(gain_part, (0, gain_rows * half - width_student))
    gain_part = gain_part.reshape(1, gain_rows, half)
    term = jnp.concatenate(
        [term, jnp.broadcast_to(gain_part, (size_z, gain_rows, half))], axis=1
    )
    term = jnp.sum(exchange(term, "z"), axis=0)
    other = lax.ppermute(term, "grp", SWAP)
    grad_factor = 1.0 / math.sqrt(tok_rows * lax.axis_size("grp") * owner_count)
    gain_grad = by_shards((term + other)[shard_rows:].reshape(-1)[:width_student]) * grad_factor
    term, other = term[:shard_rows] * grad_factor, other[:shard_rows] * grad_factor
    align_grad = jnp.where(
        core == 0,
        jnp.concatenate([term, other], axis=1),
        jnp.concatenate([other, term], axis=1),
    )

    token_loss = jnp.mean(distance * distance, axis=-1)
    gain_inner = normed_grad * gain_axes
    input_grad = by_shards(
        (
            scale_rows
            * (gain_inner - unit_rows * jnp.mean(gain_inner * unit_rows, axis=-1, keepdims=True))
        ).astype(jnp.bfloat16)
    )
    return (token_loss, input_grad, gain_grad, align_grad)


def solution(mesh):
    grid = Mesh(mesh.devices.reshape((mesh.devices.shape[0],) + DEV_SHAPE), ("grp",) + DEV)
    tokens = ("grp",) + DEV
    placed = (
        P(tokens, None),
        P(tokens, None),
        P(tokens, None),
        P(DEV, None, None),
        P(DEV, None, None),
        P(tokens),
        P(tokens, None),
        P(),
        P(DEV, None),
    )
    return jax.shard_map(
        body,
        mesh=grid,
        in_specs=placed,
        out_specs=(P(tokens), P(tokens, None), P(), P(DEV, None)),
        check_vma=False,
    )
```
